512 devices in a mesh: dp: 32 (over y, z_hi, core), tensor: 16 (over z_lo, x).
Axes of the slice: x: 4, y: 8, z: 8 (z_hi: 2, z_lo: 4; z = z_hi * 4 + z_lo), core: 2. Of those that a mesh axis runs over, the one named last changes fastest.
Arguments:
- text_feats: bfloat16 [16384, 1152], P('dp', 'tensor'), may hold values from -4 to 4
- image_feats: bfloat16 [16384, 1152], P('dp', 'tensor'), may hold values from -4 to 4
- group_ids: int32 [16384], replicated, may hold values from 0 to 8191
- log_scale: float32 [1], replicated, may hold values from 4.5 to 4.8
- bias: float32 [1], replicated, may hold values from -13 to -11
Outputs:
- text_grad: float32 [16384, 1152], P('dp', 'tensor')
- image_grad: float32 [16384, 1152], P(('dp', 'tensor'))
The draws below stay inside these ranges and needn't reach their ends.
All inputs are finite; a program needn't handle non-finite values.
Results may differ from the reference program's by a relative error of at most 0.0041.
Values may be sent and summed in bfloat16 or wider, within the bound.
A program may use at most 64 MiB of HBM per device.

```python
import math
import jax
import jax.numpy as jnp
from jax import lax

D = 1152
IMG_DEV = 32
BATCH = 16384
GROUPS = 8192
N_TENSOR = 16


topic_weight = math.sqrt(0.1)


paired_weight = math.sqrt(0.1)


noise_weight = math.sqrt(0.8)


feature_scale = 0.3


def shared_parts(key):
    topic_key, table_key, paired_key = jax.random.split(key, 3)
    topic_count = max(BATCH // 64, 1)
    topic_of = jax.random.randint(topic_key, (BATCH,), 0, topic_count)
    table = jnp.clip(jax.random.normal(table_key, (topic_count, D), jnp.float32), -4.0, 4.0)
    paired = jnp.clip(jax.random.normal(paired_key, (BATCH, D), jnp.float32), -4.0, 4.0)
    return (table[topic_of], paired)


def combine_parts(topical, paired, own_noise, row_scales):
    mixed = topic_weight * topical + paired_weight * paired + noise_weight * own_noise
    return (feature_scale * row_scales[:, None] * mixed).astype(jnp.bfloat16)


def draw_text_feats(key, part):
    topical, paired = shared_parts(key)
    key = jax.random.fold_in(key, 7)
    noise_key = jax.random.fold_in(key, 0)
    own_noise = jnp.clip(jax.random.normal(noise_key, (BATCH, D), jnp.float32), -4.0, 4.0)
    row_scales = jnp.ones((BATCH,), jnp.float32)
    return combine_parts(topical, paired, own_noise, row_scales)


def draw_image_feats(key, part):
    topical, paired = shared_parts(key)
    key = jax.random.fold_in(key, 13)
    noise_key = jax.random.fold_in(key, 0)
    own_noise = jnp.clip(jax.random.normal(noise_key, (BATCH, D), jnp.float32), -4.0, 4.0)
    row_scales = jnp.ones((BATCH,), jnp.float32)
    return combine_parts(topical, paired, own_noise, row_scales)


def set_ends(drawn, own_key, least, top_value):
    longest = drawn.shape.index(max(drawn.shape))
    spots = []
    for shift in (0, 1):
        where = [jax.random.randint(jax.random.fold_in(own_key, axis), (), 0, length) for axis, length in enumerate(drawn.shape)]
        where[longest] = (where[longest] + shift) % drawn.shape[longest]
        spots.append(tuple(where))
    return drawn.at[spots[0]].set(least).at[spots[1]].set(top_value)


def setup_inputs(seed: int = 0) -> dict:
    streams_of = jax.random.split(jax.random.key(seed), 6)
    text_feats = draw_text_feats(jax.random.fold_in(streams_of[5], 71), 0)
    image_feats = draw_image_feats(jax.random.fold_in(streams_of[5], 71), 0)
    group_ids = set_ends(jax.random.randint(streams_of[2], (BATCH,), 0, GROUPS), jax.random.fold_in(streams_of[2], 1), 0, GROUPS - 1).astype(jnp.int32)
    log_scale = jnp.clip(jax.random.uniform(streams_of[3], (1,), jnp.float32, 4.5, 4.8), 4.5, 4.8)
    bias = jnp.clip(jax.random.uniform(streams_of[4], (1,), jnp.float32, -13.0, -11.0), -13.0, -11.0)
    return dict(text_feats=text_feats, image_feats=image_feats, group_ids=group_ids, log_scale=log_scale, bias=bias)


def normalize(rows):
    wide = rows.astype(jnp.float32)
    inverse = lax.rsqrt(lax.optimization_barrier(jnp.sum(wide * wide, axis=1, keepdims=True)) + 1e-06)
    return (wide * inverse, inverse)

def unit_back(grad_hat, unit, inverse):
    return (grad_hat - unit * lax.optimization_barrier(jnp.sum(unit * grad_hat, axis=1, keepdims=True))) * inverse

def reference(text_feats, image_feats, group_ids, log_scale, bias):
    scale = jnp.exp(log_scale[0])
    offset = bias[0]
    text_unit, text_inverse = normalize(text_feats)
    image_unit, image_inverse = normalize(image_feats)
    text_hat = text_unit.astype(jnp.bfloat16)
    image_hat = image_unit.astype(jnp.bfloat16)
    block = IMG_DEV * N_TENSOR
    blocks = BATCH // block

    def visit(pushed, index):
        start = (index * block).astype(jnp.int32)
        rows_hat = lax.dynamic_slice_in_dim(text_hat, start, block, 0)
        rows_unit = lax.dynamic_slice_in_dim(text_unit, start, block, 0)
        rows_inverse = lax.dynamic_slice_in_dim(text_inverse, start, block, 0)
        rows_groups = lax.dynamic_slice_in_dim(group_ids, start, block, 0)
        logits = scale * lax.dot_general(rows_hat, image_hat, (((1,), (1,)), ((), ())), preferred_element_type=jnp.float32) + offset
        sign = jnp.where(rows_groups[:, None] == group_ids[None, :], jnp.float32(1.0), jnp.float32(-1.0))
        slope = (-sign * jax.nn.sigmoid(-sign * logits)).astype(jnp.bfloat16)
        text_push = scale * jnp.dot(slope, image_hat, preferred_element_type=jnp.float32)
        rows_grad = unit_back(text_push, rows_unit, rows_inverse)
        pushed = pushed + scale * lax.dot_general(slope, rows_hat, (((0,), (0,)), ((), ())), preferred_element_type=jnp.float32)
        return (pushed, rows_grad)
    pushed, text_grads = lax.scan(visit, jnp.zeros((BATCH, D), jnp.float32), jnp.arange(blocks, dtype=jnp.int32))
    text_grad = text_grads.reshape(BATCH, D)
    image_grad = unit_back(pushed, image_unit, image_inverse)
    return (text_grad, image_grad)
```

```python
import jax
import jax.numpy as jnp
from jax import lax
from jax.sharding import PartitionSpec as P


def normalize(rows):
    wide = rows.astype(jnp.float32)
    inverse = lax.rsqrt(jnp.sum(wide * wide, axis=1, keepdims=True) + 1e-06)
    return (wide * inverse, inverse)


def unit_back(grad_hat, unit, inverse):
    return (grad_hat - unit * jnp.sum(unit * grad_hat, axis=1, keepdims=True)) * inverse


def body(text_feats, image_feats, group_ids, log_scale, bias):
    scale = jnp.exp(log_scale[0])
    offset = bias[0]
    n_dp = lax.axis_size("dp")
    dp = lax.axis_index("dp")
    tensor = lax.axis_index("tensor")
    feats = jnp.stack([text_feats, image_feats])
    rows = lax.all_to_all(feats, "tensor", split_axis=1, concat_axis=2, tiled=True)
    text_unit, text_inverse = normalize(rows[0])
    image_unit, image_inverse = normalize(rows[1])
    width = rows.shape[1]
    count = text_feats.shape[0]
    text_hat = lax.all_gather(text_unit.astype(jnp.bfloat16), "tensor", axis=0, tiled=True)
    image_hat = lax.all_gather(image_unit.astype(jnp.bfloat16), "dp", axis=0, tiled=True)
    text_groups = lax.dynamic_slice_in_dim(group_ids, dp * count, count, 0)
    image_groups = lax.dynamic_slice_in_dim(
        group_ids.reshape(n_dp, count), tensor * width, width, 1
    ).reshape(-1)
    logits = (
        scale
        * lax.dot_general(
            image_hat, text_hat, (((1,), (1,)), ((), ())), preferred_element_type=jnp.float32
        )
        + offset
    )
    sign = jnp.where(
        image_groups[:, None] == text_groups[None, :], jnp.float32(1.0), jnp.float32(-1.0)
    )
    slope = (-sign * jax.nn.sigmoid(-sign * logits)).astype(jnp.bfloat16)
    image_push = scale * jnp.dot(slope, text_hat, preferred_element_type=jnp.float32)
    text_push = scale * lax.dot_general(
        slope, image_hat, (((0,), (0,)), ((), ())), preferred_element_type=jnp.float32
    )
    image_push = lax.psum_scatter(image_push, "dp", scatter_dimension=0, tiled=True)
    text_push = lax.psum_scatter(text_push, "tensor", scatter_dimension=0, tiled=True)
    image_grad = unit_back(image_push, image_unit, image_inverse)
    text_grad = unit_back(text_push, text_unit, text_inverse)
    text_grad = lax.all_to_all(text_grad, "tensor", split_axis=1, concat_axis=0, tiled=True)
    return (text_grad, image_grad)


def solution(mesh):
    placed = (P("dp", "tensor"), P("dp", "tensor"), P(), P(), P())
    return jax.shard_map(
        body,
        mesh=mesh,
        in_specs=placed,
        out_specs=(P("dp", "tensor"), P(("dp", "tensor"), None)),
        check_vma=False,
    )
```

```python
import jax
import jax.numpy as jnp
from jax import lax
from jax.experimental import pallas as pl
from jax.experimental.pallas import tpu as pltpu
from jax.sharding import PartitionSpec as P

MESH = pl.DeviceIdType.MESH
F32 = jnp.float32
BF16 = jnp.bfloat16

D = 1152
W = 32
NT = 16
C = D // NT
COPIES = 160

PLACE = {0: 0, 1: 1, 7: 2, 2: 3, 6: 4, 3: 5, 5: 6, 4: 7}


def device_at(y, z, core, x):
    return (y * 4 + (z // 4) * 2 + core, (z % 4) * 4 + x)


def kernel(
    text_ref, image_ref, ids_ref, log_scale_ref, bias_ref,
    text_out, image_out,
    text_slabs, image_slabs, rows32, text_unit, image_unit,
    txt, img, text_ids, image_ids, slopes,
    text_sum, chain_out, chain_in, pair_out, pair_in,
    image_sum, core_out, core_in, x_out, x_in, z_out, z_in, slices,
    send_sem, recv_sem, local_sem,
):
    dp, tensor = lax.axis_index("dp"), lax.axis_index("tensor")
    y, core = dp // 4, dp % 2
    z = ((dp // 2) % 2) * 4 + tensor // 4
    x = tensor % 4
    parity = z % 2

    def along(dy=0, dz=0, dx=0, flip=False):
        return device_at((y + dy) % 8, (z + dz) % 8, (1 - core) if flip else core, (x + dx) % 4)

    z_mate = device_at(y, z + 1 - 2 * parity, core, x)
    core_mate = along(flip=True)

    def mate(k):
        return (dp, (tensor + k) % NT)

    copies = []

    def remote(src, dst, device):
        index = len(copies)
        copy = pltpu.make_async_remote_copy(
            src_ref=src, dst_ref=dst, send_sem=send_sem.at[index], recv_sem=recv_sem.at[index],
            device_id=device, device_id_type=MESH,
        )
        copies.append(copy)
        copy.start()
        return copy

    barrier = pltpu.get_barrier_semaphore()
    greeted = [mate(k) for k in range(1, NT)]
    greeted += [core_mate, along(dy=1), along(dy=7), along(dz=4)]
    outside = device_at(y, (z + 2 + 4 * (1 - (z % 4) // 2)) % 8, core, x)
    greeted += [outside]
    for device in greeted:
        pl.semaphore_signal(barrier, inc=1, device_id=device, device_id_type=MESH)

    own_rows = pl.ds(pl.multiple_of(tensor * W, W), W)
    own_text = pltpu.make_async_copy(text_ref.at[own_rows], text_slabs.at[tensor], local_sem.at[0])
    own_image = pltpu.make_async_copy(image_ref.at[own_rows], image_slabs.at[tensor], local_sem.at[1])
    own_text.start()
    own_image.start()

    def id_row(y_at, z_at, core_at):
        at = (y_at * 4 + (z_at // 4) * 2 + core_at) * 4 + z_at % 4
        return ids_ref[pl.ds(at, 1), :]

    lane = lax.broadcasted_iota(jnp.int32, (W, 128), 1)
    row = lax.broadcasted_iota(jnp.int32, (W, 128), 0)
    own_lane = lane == row + x * W
    for r, place in PLACE.items():
        for p in range(2):
            z_at = z if p == 0 else z + 1 - 2 * parity
            ids = jnp.broadcast_to(id_row((y + r) % 8, z_at, core), (W, 128))
            at = (place * 2 + p) * W
            text_ids[at : at + W, :] = jnp.sum(
                jnp.where(own_lane, ids, 0), axis=1, keepdims=True
            )
    for c in range(2):
        for q in range(4):
            ids = id_row(y, (z + 2 * q) % 8, core if c == 0 else 1 - core)
            turned = ids
            for k in range(1, 4):
                rolled = jnp.concatenate([ids[:, k * W :], ids[:, : k * W]], axis=1)
                turned = jnp.where(x == k, rolled, turned)
            at = (c * 4 + q) * 128
            image_ids[:, at : at + 128] = turned

    scale = jnp.exp(jnp.full((1, 128), log_scale_ref[0], F32))[:, :1]
    offset = bias_ref[0]

    pl.semaphore_wait(barrier, len(greeted))

    def exchange(feats, slabs):
        out = []
        for k in range(1, NT):
            there = (tensor + k) % NT
            out.append(
                remote(
                    feats.at[pl.ds(pl.multiple_of(there * W, W), W)], slabs.at[tensor], mate(k)
                )
            )
        return out

    def normalize(slabs, unit_ref):
        total = jnp.zeros((W, 1), F32)
        for j in range(NT):
            wide = slabs[j].astype(F32)
            rows32[:, j * C : (j + 1) * C] = wide
            total = total + jnp.sum(wide * wide, axis=1, keepdims=True)
        inverse = lax.rsqrt(total + 1e-06)
        unit = rows32[...] * inverse
        unit_ref[...] = unit
        return unit.astype(BF16), inverse

    text_pieces = exchange(text_ref, text_slabs)
    image_pieces = exchange(image_ref, image_slabs)

    own_text.wait()
    for copy in text_pieces:
        copy.wait_recv()
    hat, text_inverse = normalize(text_slabs, text_unit)
    txt[0, 0] = hat

    def text_slot(r, p):
        return txt.at[PLACE[r], p]

    def forward(r, p):
        arrive = {}
        if r == 0 or (r > 4 and (r > 5 or p == 0)):
            arrive[(r - 1) % 8] = remote(text_slot(r, p), text_slot((r - 1) % 8, p), along(dy=1))
        if r == 0 or (r < 4 and (r < 3 or p == 1)):
            arrive[r + 1] = remote(text_slot(r, p), text_slot(r + 1, p), along(dy=7))
        return arrive

    pair = remote(text_slot(0, 0), text_slot(0, 1), z_mate)
    waiting = {(r, 0): copy for r, copy in forward(0, 0).items()}

    def text_step(r, p):
        waiting.pop((r, p)).wait_recv()
        waiting.update({(s, p): copy for s, copy in forward(r, p).items()})

    own_image.wait()
    for copy in image_pieces:
        copy.wait_recv()
    hat, image_inverse = normalize(image_slabs, image_unit)
    img[0, 0, 0] = hat
    z_wait = {}
    x_wait = {}
    for q in (1, 3, 2):
        z_wait[q] = remote(img.at[0, 0, 0], img.at[0, q, 0], along(dz=-2 * q))

    def spread_x(q):
        for k in (1, 3, 2):
            x_wait[(q, k)] = remote(img.at[0, q, 0], img.at[0, q, k], along(dx=-k))

    core_wait = {}

    def to_core(q):
        for k in (1, 3, 2):
            x_wait.pop((q, k)).wait_recv()
        core_wait[q] = remote(img.at[0, q], img.at[1, q], core_mate)

    spread_x(0)
    pair.wait_recv()
    waiting.update({(s, 1): copy for s, copy in forward(0, 1).items()})
    text_step(7, 0)
    text_step(1, 0)
    for q in (1, 3):
        z_wait[q].wait_recv()
        spread_x(q)
    text_step(7, 1)
    text_step(1, 1)
    z_wait[2].wait_recv()
    spread_x(2)
    text_step(6, 0)
    text_step(2, 0)
    to_core(0)
    text_step(6, 1)
    text_step(2, 1)
    to_core(1)
    text_step(5, 0)
    text_step(3, 1)
    to_core(3)
    text_step(5, 1)
    text_step(3, 0)
    to_core(2)

    def tile(batch, c, half):
        rows = txt[4 * batch : 4 * batch + 4].reshape(256, D)
        cols = img[c, 2 * half : 2 * half + 2].reshape(256, D)
        at = c * 512 + half * 256
        logits = (
            scale
            * lax.dot_general(rows, cols, (((1,), (1,)), ((), ())), preferred_element_type=F32)
            + offset
        )
        same = text_ids[batch * 256 : batch * 256 + 256, :] == image_ids[:, at : at + 256]
        share = 1.0 / (1.0 + jnp.exp(jnp.where(same, logits, -logits)))
        slopes[batch * 256 : batch * 256 + 256, at : at + 256] = jnp.where(
            same, -share, share
        ).astype(BF16)

    def text_push(batch):
        push = jnp.dot(
            slopes[batch * 256 : batch * 256 + 256, :], img[...].reshape(1024, D),
            preferred_element_type=F32,
        )
        text_sum[4 * batch : 4 * batch + 4] = push.reshape(4, 2, W, D)

    for q in range(4):
        core_wait[q].wait_recv()
    for c in range(2):
        for half in range(2):
            tile(0, c, half)
    text_push(0)
    text_step(4, 0)
    text_step(4, 1)
    for c in range(2):
        for half in range(2):
            tile(1, c, half)
    text_push(1)

    chains = (
        (0, 0, (4, 3, 2, 1)),
        (1, 1, (4, 5, 6, 7)),
        (0, 1, (3, 2, 1)),
        (1, 0, (5, 6, 7)),
    )
    arrived = {}

    def chain_step(number, hop):
        way, p, slots = chains[number]
        part = text_sum[PLACE[slots[hop]], p]
        if hop:
            arrived[number].wait_recv()
            part = part + chain_in[number, hop - 1].astype(F32)
        chain_out[number, hop] = part.astype(BF16)
        arrived[number] = remote(
            chain_out.at[number, hop], chain_in.at[number, hop], along(dy=1 if way == 0 else 7)
        )

    for number in range(4):
        chain_step(number, 0)

    def image_push(c, half):
        at = c * 512 + half * 256
        return lax.dot_general(
            slopes[:, at : at + 256], txt[...].reshape(512, D),
            (((0,), (0,)), ((), ())), preferred_element_type=F32,
        ).reshape(2, 4, W, D)

    core_sums = []
    for half in (1, 0):
        core_out[2 * half : 2 * half + 2] = image_push(1, half).astype(BF16)
        core_sums.append(
            remote(core_out.at[pl.ds(2 * half, 2)], core_in.at[pl.ds(2 * half, 2)], core_mate)
        )
    for number in range(4):
        chain_step(number, 1)
    x_sums = {}
    z_sums = {}

    def x_send(q):
        for k in (2, 1, 3):
            x_out[q, k] = (image_sum[q, k] + core_in[q, k].astype(F32)).astype(BF16)
            x_sums[(q, k)] = remote(x_out.at[q, k], x_in.at[q, k], along(dx=k))

    def z_part(q):
        part = image_sum[q, 0] + core_in[q, 0].astype(F32)
        for k in (2, 1, 3):
            x_sums[(q, k)].wait_recv()
            part = part + x_in[q, k].astype(F32)
        return part

    def z_send(q):
        z_out[q] = z_part(q).astype(BF16)
        z_sums[q] = remote(z_out.at[q], z_in.at[q], along(dz=2 * q))

    for number, half in enumerate((1, 0)):
        image_sum[2 * half : 2 * half + 2] = image_push(0, half)
        core_sums[number].wait_recv()
        x_send(2 * half + 0)
        x_send(2 * half + 1)
    for number in range(4):
        chain_step(number, 2)
    z_send(2)
    z_send(3)
    for number in range(2):
        chain_step(number, 3)
    z_send(1)

    def gathered(p):
        total = text_sum[0, p]
        for number, (way, chain_p, slots) in enumerate(chains):
            if chain_p == p:
                arrived[number].wait_recv()
                total = total + chain_in[number, len(slots) - 1].astype(F32)
        return total

    def unit_back(push, unit, inverse):
        push = push * scale
        return (push - unit * jnp.sum(unit * push, axis=1, keepdims=True)) * inverse

    pair_out[...] = gathered(1).astype(BF16)
    mate_sum = remote(pair_out, pair_in, z_mate)
    push = gathered(0)
    mate_sum.wait_recv()
    grad = unit_back(push + pair_in[...].astype(F32), text_unit[...], text_inverse)
    for j in range(NT):
        slices[j] = grad[:, j * C : (j + 1) * C]
    back = []
    for k in range(1, NT):
        back.append(
            remote(slices.at[(tensor + k) % NT], text_out.at[own_rows], mate(k))
        )
    text_out[own_rows, :] = slices[tensor]

    push = z_part(0)
    for q in (1, 3, 2):
        z_sums[q].wait_recv()
        push = push + z_in[q].astype(F32)
    image_out[...] = unit_back(push, image_unit[...], image_inverse)

    for copy in back:
        copy.wait_recv()
    for copy in copies:
        copy.wait_send()


def body(text_feats, image_feats, group_ids, log_scale, bias):
    anywhere = pl.BlockSpec(memory_space=pl.ANY)
    vmem = pl.BlockSpec(memory_space=pltpu.VMEM)
    smem = pl.BlockSpec(memory_space=pltpu.SMEM)
    block = (W, D)
    return pl.pallas_call(
        kernel,
        out_shape=(
            jax.ShapeDtypeStruct((NT * W, C), F32),
            jax.ShapeDtypeStruct(block, F32),
        ),
        in_specs=[anywhere, anywhere, vmem, smem, smem],
        out_specs=(vmem, vmem),
        scratch_shapes=[
            pltpu.VMEM((NT, W, C), BF16),
            pltpu.VMEM((NT, W, C), BF16),
            pltpu.VMEM(block, F32),
            pltpu.VMEM(block, F32),
            pltpu.VMEM(block, F32),
            pltpu.VMEM((8, 2) + block, BF16),
            pltpu.VMEM((2, 4, 4) + block, BF16),
            pltpu.VMEM((512, 1), jnp.int32),
            pltpu.VMEM((1, 1024), jnp.int32),
            pltpu.VMEM((512, 1024), BF16),
            pltpu.VMEM((8, 2) + block, F32),
            pltpu.VMEM((4, 4) + block, BF16),
            pltpu.VMEM((4, 4) + block, BF16),
            pltpu.VMEM(block, BF16),
            pltpu.VMEM(block, BF16),
            pltpu.VMEM((4, 4) + block, F32),
            pltpu.VMEM((4, 4) + block, BF16),
            pltpu.VMEM((4, 4) + block, BF16),
            pltpu.VMEM((4, 4) + block, BF16),
            pltpu.VMEM((4, 4) + block, BF16),
            pltpu.VMEM((4,) + block, BF16),
            pltpu.VMEM((4,) + block, BF16),
            pltpu.VMEM((NT, W, C), F32),
            pltpu.SemaphoreType.DMA((COPIES,)),
            pltpu.SemaphoreType.DMA((COPIES,)),
            pltpu.SemaphoreType.DMA((2,)),
        ],
        compiler_params=pltpu.CompilerParams(
            collective_id=0, has_side_effects=True, vmem_limit_bytes=50 * 2**20
        ),
    )(text_feats, image_feats, group_ids.reshape(128, 128), log_scale, bias)


def solution(mesh):
    placed = (P("dp", "tensor"), P("dp", "tensor"), P(), P(), P())
    return jax.shard_map(
        body,
        mesh=mesh,
        in_specs=placed,
        out_specs=(P("dp", "tensor"), P(("dp", "tensor"), None)),
        check_vma=False,
    )
```

```python
import jax
import jax.numpy as jnp
from jax import lax
from jax.experimental import pallas as pl
from jax.experimental.pallas import tpu as pltpu
from jax.sharding import PartitionSpec as P

MESH = pl.DeviceIdType.MESH
F32 = jnp.float32
BF16 = jnp.bfloat16

D = 1152
W = 32
NT = 16
C = D // NT
COPIES = 160

PLACE = {0: 0, 1: 1, 7: 2, 2: 3, 6: 4, 3: 5, 5: 6, 4: 7}


def device_at(y, z, core, x):
    return (y * 4 + (z // 4) * 2 + core, (z % 4) * 4 + x)


def kernel(
    text_hbm, image_hbm, ids_hbm, log_scale_ref, bias_ref,
    text_out, image_out,
    text_own, image_own, ids, cols_out, cols_in, turned, rows_out, rows_in,
    rows32, text_unit, image_unit,
    txt, img, text_ids, image_ids, slopes,
    text_sum, chain_out, chain_in, pair_out, pair_in,
    image_sum, core_out, core_in, x_out, x_in, z_out, z_in,
    grad_out, grad_in, back_out,
    send_sem, recv_sem, local_sem,
):
    dp, tensor = lax.axis_index("dp"), lax.axis_index("tensor")
    y, core = dp // 4, dp % 2
    z = ((dp // 2) % 2) * 4 + tensor // 4
    x = tensor % 4
    parity = z % 2

    def along(dy=0, dz=0, dx=0, flip=False):
        return device_at((y + dy) % 8, (z + dz) % 8, (1 - core) if flip else core, (x + dx) % 4)

    z_lo = z % 4
    z_mate = device_at(y, z + 1 - 2 * parity, core, x)
    core_mate = along(flip=True)

    def z_run(k):
        return device_at(y, z - z_lo + (z_lo + k) % 4, core, x)

    copies = []

    def remote(src, dst, device):
        index = len(copies)
        copy = pltpu.make_async_remote_copy(
            src_ref=src, dst_ref=dst, send_sem=send_sem.at[index], recv_sem=recv_sem.at[index],
            device_id=device, device_id_type=MESH,
        )
        copies.append(copy)
        copy.start()
        return copy

    loads = [
        pltpu.make_async_copy(src, dst, local_sem.at[n])
        for n, (src, dst) in enumerate(
            ((text_hbm, text_own), (image_hbm, image_own), (ids_hbm, ids))
        )
    ]
    for load in loads:
        load.start()

    barrier = pltpu.get_barrier_semaphore()
    greeted = [z_run(k) for k in (1, 2, 3)] + [along(dx=k) for k in (1, 2, 3)]
    greeted += [core_mate, along(dy=1), along(dy=7), along(dz=4)]
    greeted += [device_at(y, (z + 2 + 4 * (1 - z_lo // 2)) % 8, core, x)]
    for device in greeted:
        pl.semaphore_signal(barrier, inc=1, device_id=device, device_id_type=MESH)

    for load in loads:
        load.wait()
    for kind, own in enumerate((text_own, image_own)):
        for run in range(4):
            piece = own[:, run * 128 : run * 128 + 128].astype(F32)
            cols_out[run, kind] = jnp.concatenate([piece, jnp.zeros((8, 128), F32)], axis=0).astype(BF16)
    pl.semaphore_wait(barrier, len(greeted))
    run_pieces = [
        remote(cols_out.at[(z_lo + k) % 4], cols_in.at[z_lo], z_run(k)) for k in (1, 3, 2)
    ]
    cols_in[z_lo] = cols_out[z_lo]

    def id_row(y_at, z_at, core_at):
        at = (y_at * 4 + (z_at // 4) * 2 + core_at) * 4 + z_at % 4
        return ids[pl.ds(at, 1), :]

    lane = lax.broadcasted_iota(jnp.int32, (W, 128), 1)
    row = lax.broadcasted_iota(jnp.int32, (W, 128), 0)
    own_lane = lane == row + x * W
    for r, place in PLACE.items():
        for p in range(2):
            z_at = z if p == 0 else z + 1 - 2 * parity
            here = jnp.broadcast_to(id_row((y + r) % 8, z_at, core), (W, 128))
            at = (place * 2 + p) * W
            text_ids[at : at + W, :] = jnp.sum(
                jnp.where(own_lane, here, 0), axis=1, keepdims=True
            )
    for c in range(2):
        for q in range(4):
            here = id_row(y, (z + 2 * q) % 8, core if c == 0 else 1 - core)
            from_x = here
            for k in range(1, 4):
                rolled = jnp.concatenate([here[:, k * W :], here[:, : k * W]], axis=1)
                from_x = jnp.where(x == k, rolled, from_x)
            at = (c * 4 + q) * 128
            image_ids[:, at : at + 128] = from_x

    scale = jnp.exp(jnp.full((1, 128), log_scale_ref[0], F32))[:, :1]
    offset = bias_ref[0]

    for copy in run_pieces:
        copy.wait_recv()
    for kind in range(2):
        for run in range(4):
            turned[run * C : run * C + C, :] = cols_in[run, kind].astype(F32)[:C]
        turned[4 * C :, :] = jnp.zeros((384 - 4 * C, 128), F32)
        rows_out[:, kind] = turned[...].T.astype(BF16).reshape(4, W, 384)
    x_pieces = [
        remote(rows_out.at[(x + k) % 4], rows_in.at[x], along(dx=k)) for k in (1, 3, 2)
    ]
    rows_in[x] = rows_out[x]
    for copy in x_pieces:
        copy.wait_recv()

    def normalize(kind, unit_ref):
        total = jnp.zeros((W, 1), F32)
        for j in range(4):
            wide = rows_in[j, kind].astype(F32)[:, : 4 * C]
            rows32[:, j * 4 * C : (j + 1) * 4 * C] = wide
            total = total + jnp.sum(wide * wide, axis=1, keepdims=True)
        inverse = lax.rsqrt(total + 1e-06)
        unit = rows32[...] * inverse
        unit_ref[...] = unit
        return unit.astype(BF16), inverse

    hat, text_inverse = normalize(0, text_unit)
    txt[0, 0] = hat

    def text_slot(r, p):
        return txt.at[PLACE[r], p]

    def forward(r, p):
        arrive = {}
        if r == 0 or (r > 4 and (r > 5 or p == 0)):
            arrive[(r - 1) % 8] = remote(text_slot(r, p), text_slot((r - 1) % 8, p), along(dy=1))
        if r == 0 or (r < 4 and (r < 3 or p == 1)):
            arrive[r + 1] = remote(text_slot(r, p), text_slot(r + 1, p), along(dy=7))
        return arrive

    pair = remote(text_slot(0, 0), text_slot(0, 1), z_mate)
    waiting = {(r, 0): copy for r, copy in forward(0, 0).items()}

    def text_step(r, p):
        waiting.pop((r, p)).wait_recv()
        waiting.update({(s, p): copy for s, copy in forward(r, p).items()})

    hat, image_inverse = normalize(1, image_unit)
    img[0, 0, 0] = hat
    z_wait = {}
    x_wait = {}
    for q in (1, 3, 2):
        z_wait[q] = remote(img.at[0, 0, 0], img.at[0, q, 0], along(dz=-2 * q))

    def spread_x(q):
        for k in (1, 3, 2):
            x_wait[(q, k)] = remote(img.at[0, q, 0], img.at[0, q, k], along(dx=-k))

    core_wait = {}

    def to_core(q):
        for k in (1, 3, 2):
            x_wait.pop((q, k)).wait_recv()
        core_wait[q] = remote(img.at[0, q], img.at[1, q], core_mate)

    spread_x(0)
    pair.wait_recv()
    waiting.update({(s, 1): copy for s, copy in forward(0, 1).items()})
    text_step(7, 0)
    text_step(1, 0)
    for q in (1, 3):
        z_wait[q].wait_recv()
        spread_x(q)
    text_step(7, 1)
    text_step(1, 1)
    z_wait[2].wait_recv()
    spread_x(2)
    text_step(6, 0)
    text_step(2, 0)
    to_core(0)
    text_step(6, 1)
    text_step(2, 1)
    to_core(1)
    text_step(5, 0)
    text_step(3, 1)
    to_core(3)
    text_step(5, 1)
    text_step(3, 0)
    to_core(2)

    def tile(batch, c, half):
        rows = txt[4 * batch : 4 * batch + 4].reshape(256, D)
        cols = img[c, 2 * half : 2 * half + 2].reshape(256, D)
        at = c * 512 + half * 256
        logits = (
            scale
            * lax.dot_general(rows, cols, (((1,), (1,)), ((), ())), preferred_element_type=F32)
            + offset
        )
        same = text_ids[batch * 256 : batch * 256 + 256, :] == image_ids[:, at : at + 256]
        share = 1.0 / (1.0 + jnp.exp(jnp.where(same, logits, -logits)))
        slopes[batch * 256 : batch * 256 + 256, at : at + 256] = jnp.where(
            same, -share, share
        ).astype(BF16)

    def text_push(batch):
        push = jnp.dot(
            slopes[batch * 256 : batch * 256 + 256, :], img[...].reshape(1024, D),
            preferred_element_type=F32,
        )
        text_sum[4 * batch : 4 * batch + 4] = push.reshape(4, 2, W, D)

    for q in range(4):
        core_wait[q].wait_recv()
    for c in range(2):
        for half in range(2):
            tile(0, c, half)
    text_push(0)
    text_step(4, 0)
    text_step(4, 1)
    for c in range(2):
        for half in range(2):
            tile(1, c, half)
    text_push(1)

    chains = (
        (0, 0, (4, 3, 2, 1)),
        (1, 1, (4, 5, 6, 7)),
        (0, 1, (3, 2, 1)),
        (1, 0, (5, 6, 7)),
    )
    arrived = {}

    def chain_step(number, hop):
        way, p, slots = chains[number]
        part = text_sum[PLACE[slots[hop]], p]
        if hop:
            arrived[number].wait_recv()
            part = part + chain_in[number, hop - 1].astype(F32)
        chain_out[number, hop] = part.astype(BF16)
        arrived[number] = remote(
            chain_out.at[number, hop], chain_in.at[number, hop], along(dy=1 if way == 0 else 7)
        )

    for number in range(4):
        chain_step(number, 0)

    def image_push(c, half):
        at = c * 512 + half * 256
        return lax.dot_general(
            slopes[:, at : at + 256], txt[...].reshape(512, D),
            (((0,), (0,)), ((), ())), preferred_element_type=F32,
        ).reshape(2, 4, W, D)

    x_sums = {}
    z_sums = {}

    def x_send(q):
        for k in (2, 1, 3):
            x_out[q, k] = (image_sum[q, k] + core_in[q, k].astype(F32)).astype(BF16)
            x_sums[(q, k)] = remote(x_out.at[q, k], x_in.at[q, k], along(dx=k))

    def z_part(q):
        part = image_sum[q, 0] + core_in[q, 0].astype(F32)
        for k in (2, 1, 3):
            x_sums[(q, k)].wait_recv()
            part = part + x_in[q, k].astype(F32)
        return part

    def z_send(q):
        z_out[q] = z_part(q).astype(BF16)
        z_sums[q] = remote(z_out.at[q], z_in.at[q], along(dz=2 * q))

    core_sums = []
    for half in (1, 0):
        core_out[2 * half : 2 * half + 2] = image_push(1, half).astype(BF16)
        core_sums.append(
            remote(core_out.at[pl.ds(2 * half, 2)], core_in.at[pl.ds(2 * half, 2)], core_mate)
        )
    for half in (1, 0):
        image_sum[2 * half : 2 * half + 2] = image_push(0, half)
    for number in range(4):
        chain_step(number, 1)
    core_sums[0].wait_recv()
    x_send(2)
    x_send(3)
    core_sums[1].wait_recv()
    x_send(1)
    x_send(0)
    for number in range(4):
        chain_step(number, 2)
    for number in range(2):
        chain_step(number, 3)
    z_send(2)
    z_send(3)

    def gathered(p):
        total = text_sum[0, p]
        for number, (way, chain_p, slots) in enumerate(chains):
            if chain_p == p:
                arrived[number].wait_recv()
                total = total + chain_in[number, len(slots) - 1].astype(F32)
        return total

    def unit_back(push, unit, inverse):
        push = push * scale
        return (push - unit * jnp.sum(unit * push, axis=1, keepdims=True)) * inverse

    pair_out[...] = gathered(1).astype(BF16)
    mate_sum = remote(pair_out, pair_in, z_mate)
    z_send(1)
    push = gathered(0)
    mate_sum.wait_recv()
    grad = unit_back(push + pair_in[...].astype(F32), text_unit[...], text_inverse)
    blank = jnp.zeros((W, 384 - 4 * C), F32)
    for j in range(4):
        grad_out[j] = jnp.concatenate([grad[:, j * 4 * C : (j + 1) * 4 * C], blank], axis=1)
    x_back = [
        remote(grad_out.at[(x + k) % 4], grad_in.at[x], along(dx=k)) for k in (1, 3, 2)
    ]
    grad_in[x] = grad_out[x]
    image_push_total = z_part(0)
    for copy in x_back:
        copy.wait_recv()
    down = grad_in[...].reshape(128, 384).T
    for run in range(4):
        back_out[run] = down[run * C : run * C + C]
    lanes = pl.ds(pl.multiple_of(z_lo * 128, 128), 128)
    z_back = [
        remote(back_out.at[(z_lo + k) % 4], text_out.at[:, lanes], z_run(k)) for k in (1, 3, 2)
    ]
    text_out[:, lanes] = back_out[z_lo]

    for q in (1, 3, 2):
        z_sums[q].wait_recv()
        image_push_total = image_push_total + z_in[q].astype(F32)
    grad = unit_back(image_push_total, image_unit[...], image_inverse)
    for j in range(4):
        for run in range(4):
            at = (j * 4 + run) * C
            image_out[:, (run * 4 + j) * C : (run * 4 + j + 1) * C] = grad[:, at : at + C]

    for copy in z_back:
        copy.wait_recv()
    for copy in copies:
        copy.wait_send()


def body(text_feats, image_feats, group_ids, log_scale, bias):
    anywhere = pl.BlockSpec(memory_space=pl.ANY)
    vmem = pl.BlockSpec(memory_space=pltpu.VMEM)
    smem = pl.BlockSpec(memory_space=pltpu.SMEM)
    block = (W, D)
    text_grad, image_grad = pl.pallas_call(
        kernel,
        out_shape=(
            jax.ShapeDtypeStruct((C, NT * W), F32),
            jax.ShapeDtypeStruct(block, F32),
        ),
        in_specs=[anywhere, anywhere, anywhere, smem, smem],
        out_specs=(vmem, vmem),
        scratch_shapes=[
            pltpu.VMEM((C, NT * W), BF16),
            pltpu.VMEM((C, NT * W), BF16),
            pltpu.VMEM((128, 128), jnp.int32),
            pltpu.VMEM((4, 2, C + 8, 128), BF16),
            pltpu.VMEM((4, 2, C + 8, 128), BF16),
            pltpu.VMEM((384, 128), F32),
            pltpu.VMEM((4, 2, W, 384), BF16),
            pltpu.VMEM((4, 2, W, 384), BF16),
            pltpu.VMEM(block, F32),
            pltpu.VMEM(block, F32),
            pltpu.VMEM(block, F32),
            pltpu.VMEM((8, 2) + block, BF16),
            pltpu.VMEM((2, 4, 4) + block, BF16),
            pltpu.VMEM((512, 1), jnp.int32),
            pltpu.VMEM((1, 1024), jnp.int32),
            pltpu.VMEM((512, 1024), BF16),
            pltpu.VMEM((8, 2) + block, F32),
            pltpu.VMEM((4, 4) + block, BF16),
            pltpu.VMEM((4, 4) + block, BF16),
            pltpu.VMEM(block, BF16),
            pltpu.VMEM(block, BF16),
            pltpu.VMEM((4, 4) + block, F32),
            pltpu.VMEM((4, 4) + block, BF16),
            pltpu.VMEM((4, 4) + block, BF16),
            pltpu.VMEM((4, 4) + block, BF16),
            pltpu.VMEM((4, 4) + block, BF16),
            pltpu.VMEM((4,) + block, BF16),
            pltpu.VMEM((4,) + block, BF16),
            pltpu.VMEM((4, W, 384), F32),
            pltpu.VMEM((4, W, 384), F32),
            pltpu.VMEM((4, C, 128), F32),
            pltpu.SemaphoreType.DMA((COPIES,)),
            pltpu.SemaphoreType.DMA((COPIES,)),
            pltpu.SemaphoreType.DMA((3,)),
        ],
        compiler_params=pltpu.CompilerParams(
            collective_id=0, has_side_effects=True, vmem_limit_bytes=50 * 2**20
        ),
    )(text_feats.T, image_feats.T, group_ids.reshape(128, 128), log_scale, bias)
    return (text_grad.T, image_grad)


def solution(mesh):
    placed = (P("dp", "tensor"), P("dp", "tensor"), P(), P(), P())
    return jax.shard_map(
        body,
        mesh=mesh,
        in_specs=placed,
        out_specs=(P("dp", "tensor"), P(("dp", "tensor"), None)),
        check_vma=False,
    )
```

```python
import jax
import jax.numpy as jnp
from jax import lax
from jax.experimental import pallas as pl
from jax.experimental.pallas import tpu as pltpu
from jax.sharding import PartitionSpec as P

MESH = pl.DeviceIdType.MESH
F32 = jnp.float32
BF16 = jnp.bfloat16

D = 1152
W = 32
NT = 16
C = D // NT
COPIES = 84

PLACE = {0: 0, 1: 1, 7: 2, 2: 3, 6: 4, 3: 5, 5: 6, 4: 7}


def device_at(y, z, core, x):
    return (y * 4 + (z // 4) * 2 + core, (z % 4) * 4 + x)


def kernel(
    text_hbm, image_hbm, ids_hbm, log_scale_ref, bias_ref,
    text_out, image_out,
    text_own, image_own, ids, cols_out, cols_in, turned, rows_out, rows_in,
    rows32, text_unit, image_unit,
    txt, img, text_ids, image_ids, slopes,
    text_sum, chain_out, chain_in, pair_out, pair_in,
    image_sum, core_out, core_in, x_out, x_in, z_out, z_in,
    grad_out, grad_in, back_out,
    send_sem, recv_sem, local_sem,
):
    dp, tensor = lax.axis_index("dp"), lax.axis_index("tensor")
    y, core = dp // 4, dp % 2
    z = ((dp // 2) % 2) * 4 + tensor // 4
    x = tensor % 4
    parity = z % 2

    def along(dy=0, dz=0, dx=0, flip=False):
        return device_at((y + dy) % 8, (z + dz) % 8, (1 - core) if flip else core, (x + dx) % 4)

    z_lo = z % 4
    z_mate = device_at(y, z + 1 - 2 * parity, core, x)
    core_mate = along(flip=True)

    def z_run(k):
        return device_at(y, z - z_lo + (z_lo + k) % 4, core, x)

    copies = []

    def remote(src, dst, device):
        index = len(copies)
        copy = pltpu.make_async_remote_copy(
            src_ref=src, dst_ref=dst, send_sem=send_sem.at[index], recv_sem=recv_sem.at[index],
            device_id=device, device_id_type=MESH,
        )
        copies.append(copy)
        copy.start()
        return copy

    loads = [
        pltpu.make_async_copy(src, dst, local_sem.at[n])
        for n, (src, dst) in enumerate(
            ((text_hbm, text_own), (image_hbm, image_own), (ids_hbm, ids))
        )
    ]
    for load in loads:
        load.start()

    barrier = pltpu.get_barrier_semaphore()
    greeted = [z_run(k) for k in (1, 2, 3)] + [along(dx=k) for k in (1, 2, 3)]
    greeted += [core_mate, along(dy=1), along(dy=7), along(dz=4)]
    greeted += [device_at(y, (z + 2 + 4 * (1 - z_lo // 2)) % 8, core, x)]
    for device in greeted:
        pl.semaphore_signal(barrier, inc=1, device_id=device, device_id_type=MESH)

    for load in loads:
        load.wait()
    for kind, own in enumerate((text_own, image_own)):
        for run in range(4):
            piece = own[:, run * 128 : run * 128 + 128].astype(F32)
            cols_out[kind, run] = jnp.concatenate([piece, jnp.zeros((8, 128), F32)], axis=0).astype(BF16)
    pl.semaphore_wait(barrier, len(greeted))
    run_pieces = []
    for kind in range(2):
        run_pieces.append([
            remote(cols_out.at[kind, (z_lo + k) % 4], cols_in.at[kind, z_lo], z_run(k))
            for k in (1, 3, 2)
        ])
        cols_in[kind, z_lo] = cols_out[kind, z_lo]

    def id_row(y_at, z_at, core_at):
        at = (y_at * 4 + (z_at // 4) * 2 + core_at) * 4 + z_at % 4
        return ids[pl.ds(at, 1), :]

    lane = lax.broadcasted_iota(jnp.int32, (W, 128), 1)
    row = lax.broadcasted_iota(jnp.int32, (W, 128), 0)
    own_lane = lane == row + x * W
    for r, place in PLACE.items():
        for p in range(2):
            z_at = z if p == 0 else z + 1 - 2 * parity
            here = jnp.broadcast_to(id_row((y + r) % 8, z_at, core), (W, 128))
            at = (place * 2 + p) * W
            text_ids[at : at + W, :] = jnp.sum(
                jnp.where(own_lane, here, 0), axis=1, keepdims=True
            )
    for c in range(2):
        for q in range(4):
            here = id_row(y, (z + 2 * q) % 8, core if c == 0 else 1 - core)
            from_x = here
            for k in range(1, 4):
                rolled = jnp.concatenate([here[:, k * W :], here[:, : k * W]], axis=1)
                from_x = jnp.where(x == k, rolled, from_x)
            at = (c * 4 + q) * 128
            image_ids[:, at : at + 128] = from_x

    scale = jnp.exp(jnp.full((1, 128), log_scale_ref[0], F32))[:, :1]
    offset = bias_ref[0]

    turned[4 * C :, :] = jnp.zeros((384 - 4 * C, 128), F32)
    x_pieces = []
    for kind in range(2):
        for copy in run_pieces[kind]:
            copy.wait_recv()
        for run in range(4):
            turned[run * C : run * C + C, :] = cols_in[kind, run].astype(F32)[:C]
        rows_out[kind] = turned[...].T.astype(BF16).reshape(4, W, 384)
        x_pieces.append([
            remote(rows_out.at[kind, (x + k) % 4], rows_in.at[kind, x], along(dx=k))
            for k in (1, 3, 2)
        ])
        rows_in[kind, x] = rows_out[kind, x]

    def normalize(kind, unit_ref):
        for copy in x_pieces[kind]:
            copy.wait_recv()
        total = jnp.zeros((W, 1), F32)
        for j in range(4):
            wide = rows_in[kind, j].astype(F32)[:, : 4 * C]
            rows32[:, j * 4 * C : (j + 1) * 4 * C] = wide
            total = total + jnp.sum(wide * wide, axis=1, keepdims=True)
        inverse = lax.rsqrt(total + 1e-06)
        unit = rows32[...] * inverse
        unit_ref[...] = unit
        return unit.astype(BF16), inverse

    hat, text_inverse = normalize(0, text_unit)
    txt[0, 0] = hat

    def text_slot(r, p):
        return txt.at[PLACE[r], p]

    def forward(r, p):
        arrive = {}
        if r == 0 or (r > 4 and (r > 5 or p == 0)):
            arrive[(r - 1) % 8] = remote(text_slot(r, p), text_slot((r - 1) % 8, p), along(dy=1))
        if r == 0 or (r < 4 and (r < 3 or p == 1)):
            arrive[r + 1] = remote(text_slot(r, p), text_slot(r + 1, p), along(dy=7))
        return arrive

    pair = remote(text_slot(0, 0), text_slot(0, 1), z_mate)
    waiting = {(r, 0): copy for r, copy in forward(0, 0).items()}

    def text_step(r, p):
        waiting.pop((r, p)).wait_recv()
        waiting.update({(s, p): copy for s, copy in forward(r, p).items()})

    hat, image_inverse = normalize(1, image_unit)
    img[0, 0, 0] = hat
    z_wait = {}
    x_wait = {}
    for q in (1, 3, 2):
        z_wait[q] = remote(img.at[0, 0, 0], img.at[0, q, 0], along(dz=-2 * q))

    def spread_x(q):
        for k in (1, 3, 2):
            x_wait[(q, k)] = remote(img.at[0, q, 0], img.at[0, q, k], along(dx=-k))

    core_wait = {}

    def to_core(q):
        for k in (1, 3, 2):
            x_wait.pop((q, k)).wait_recv()
        core_wait[q] = remote(img.at[0, q], img.at[1, q], core_mate)

    spread_x(0)
    pair.wait_recv()
    waiting.update({(s, 1): copy for s, copy in forward(0, 1).items()})
    text_step(7, 0)
    text_step(1, 0)
    for q in (1, 3):
        z_wait[q].wait_recv()
        spread_x(q)
    text_step(7, 1)
    text_step(1, 1)
    z_wait[2].wait_recv()
    spread_x(2)
    text_step(6, 0)
    text_step(2, 0)
    to_core(0)
    text_step(6, 1)
    text_step(2, 1)
    to_core(1)
    text_step(5, 0)
    text_step(3, 1)
    to_core(3)
    text_step(5, 1)
    text_step(3, 0)
    to_core(2)

    def tile(batch, c, half):
        rows = txt[4 * batch : 4 * batch + 4].reshape(256, D)
        cols = img[c, 2 * half : 2 * half + 2].reshape(256, D)
        at = c * 512 + half * 256
        logits = (
            scale
            * lax.dot_general(rows, cols, (((1,), (1,)), ((), ())), preferred_element_type=F32)
            + offset
        )
        same = text_ids[batch * 256 : batch * 256 + 256, :] == image_ids[:, at : at + 256]
        share = 1.0 / (1.0 + jnp.exp(jnp.where(same, logits, -logits)))
        slopes[batch * 256 : batch * 256 + 256, at : at + 256] = jnp.where(
            same, -share, share
        ).astype(BF16)

    def text_push(batch):
        push = jnp.dot(
            slopes[batch * 256 : batch * 256 + 256, :], img[...].reshape(1024, D),
            preferred_element_type=F32,
        )
        text_sum[4 * batch : 4 * batch + 4] = push.reshape(4, 2, W, D)

    for q in range(4):
        core_wait[q].wait_recv()
    for c in range(2):
        for half in range(2):
            tile(0, c, half)
    text_push(0)
    text_step(4, 0)
    text_step(4, 1)
    for c in range(2):
        for half in range(2):
            tile(1, c, half)
    text_push(1)

    chains = (
        (0, 0, (4, 3, 2, 1)),
        (1, 1, (4, 5, 6, 7)),
        (0, 1, (3, 2, 1)),
        (1, 0, (5, 6, 7)),
    )
    arrived = {}

    def chain_step(number, hop):
        way, p, slots = chains[number]
        part = text_sum[PLACE[slots[hop]], p]
        if hop:
            arrived[number].wait_recv()
            part = part + chain_in[number, hop - 1].astype(F32)
        chain_out[number, hop] = part.astype(BF16)
        arrived[number] = remote(
            chain_out.at[number, hop], chain_in.at[number, hop], along(dy=1 if way == 0 else 7)
        )

    chain_step(0, 0)
    chain_step(1, 0)

    def image_push(c, half):
        at = c * 512 + half * 256
        return lax.dot_general(
            slopes[:, at : at + 256], txt[...].reshape(512, D),
            (((0,), (0,)), ((), ())), preferred_element_type=F32,
        ).reshape(2, 4, W, D)

    x_sums = {}
    z_sums = {}

    def x_send(q):
        for k in (2, 1, 3):
            x_out[q, k] = (image_sum[q, k] + core_in[q, k].astype(F32)).astype(BF16)
            x_sums[(q, k)] = remote(x_out.at[q, k], x_in.at[q, k], along(dx=k))

    def z_part(q):
        part = image_sum[q, 0] + core_in[q, 0].astype(F32)
        for k in (2, 1, 3):
            x_sums[(q, k)].wait_recv()
            part = part + x_in[q, k].astype(F32)
        return part

    def z_send(q):
        z_out[q] = z_part(q).astype(BF16)
        z_sums[q] = remote(z_out.at[q], z_in.at[q], along(dz=2 * q))

    core_sums = []
    for half in (1, 0):
        core_out[2 * half : 2 * half + 2] = image_push(1, half).astype(BF16)
        core_sums.append(
            remote(core_out.at[pl.ds(2 * half, 2)], core_in.at[pl.ds(2 * half, 2)], core_mate)
        )
    chain_step(2, 0)
    chain_step(3, 0)
    for half in (1, 0):
        image_sum[2 * half : 2 * half + 2] = image_push(0, half)
    core_sums[0].wait_recv()
    x_send(2)
    chain_step(0, 1)
    chain_step(1, 1)
    x_send(3)
    core_sums[1].wait_recv()
    x_send(1)
    chain_step(2, 1)
    chain_step(3, 1)
    x_send(0)
    chain_step(0, 2)
    chain_step(1, 2)
    chain_step(2, 2)
    chain_step(3, 2)
    z_send(2)
    chain_step(0, 3)
    chain_step(1, 3)
    z_send(3)

    def gathered(p):
        total = text_sum[0, p]
        for number, (way, chain_p, slots) in enumerate(chains):
            if chain_p == p:
                arrived[number].wait_recv()
                total = total + chain_in[number, len(slots) - 1].astype(F32)
        return total

    def unit_back(push, unit, inverse):
        push = push * scale
        return (push - unit * jnp.sum(unit * push, axis=1, keepdims=True)) * inverse

    pair_out[...] = gathered(1).astype(BF16)
    mate_sum = remote(pair_out, pair_in, z_mate)
    z_send(1)
    push = gathered(0)
    mate_sum.wait_recv()
    grad = unit_back(push + pair_in[...].astype(F32), text_unit[...], text_inverse)
    blank = jnp.zeros((W, 384 - 4 * C), F32)
    for j in range(4):
        grad_out[j] = jnp.concatenate([grad[:, j * 4 * C : (j + 1) * 4 * C], blank], axis=1)
    x_back = [
        remote(grad_out.at[(x + k) % 4], grad_in.at[x], along(dx=k)) for k in (1, 3, 2)
    ]
    grad_in[x] = grad_out[x]
    image_push_total = z_part(0)
    for copy in x_back:
        copy.wait_recv()
    down = grad_in[...].reshape(128, 384).T
    for run in range(4):
        back_out[run] = down[run * C : run * C + C]
    lanes = pl.ds(pl.multiple_of(z_lo * 128, 128), 128)
    z_back = [
        remote(back_out.at[(z_lo + k) % 4], text_out.at[:, lanes], z_run(k)) for k in (1, 3, 2)
    ]
    text_out[:, lanes] = back_out[z_lo]

    for q in (1, 3, 2):
        z_sums[q].wait_recv()
        image_push_total = image_push_total + z_in[q].astype(F32)
    grad = unit_back(image_push_total, image_unit[...], image_inverse)
    for j in range(4):
        for run in range(4):
            at = (j * 4 + run) * C
            image_out[:, (run * 4 + j) * C : (run * 4 + j + 1) * C] = grad[:, at : at + C]

    for copy in z_back:
        copy.wait_recv()
    for copy in copies:
        copy.wait_send()


def body(text_feats, image_feats, group_ids, log_scale, bias):
    anywhere = pl.BlockSpec(memory_space=pl.ANY)
    vmem = pl.BlockSpec(memory_space=pltpu.VMEM)
    smem = pl.BlockSpec(memory_space=pltpu.SMEM)
    block = (W, D)
    text_grad, image_grad = pl.pallas_call(
        kernel,
        out_shape=(
            jax.ShapeDtypeStruct((C, NT * W), F32),
            jax.ShapeDtypeStruct(block, F32),
        ),
        in_specs=[anywhere, anywhere, anywhere, smem, smem],
        out_specs=(vmem, vmem),
        scratch_shapes=[
            pltpu.VMEM((C, NT * W), BF16),
            pltpu.VMEM((C, NT * W), BF16),
            pltpu.VMEM((128, 128), jnp.int32),
            pltpu.VMEM((2, 4, C + 8, 128), BF16),
            pltpu.VMEM((2, 4, C + 8, 128), BF16),
            pltpu.VMEM((384, 128), F32),
            pltpu.VMEM((2, 4, W, 384), BF16),
            pltpu.VMEM((2, 4, W, 384), BF16),
            pltpu.VMEM(block, F32),
            pltpu.VMEM(block, F32),
            pltpu.VMEM(block, F32),
            pltpu.VMEM((8, 2) + block, BF16),
            pltpu.VMEM((2, 4, 4) + block, BF16),
            pltpu.VMEM((512, 1), jnp.int32),
            pltpu.VMEM((1, 1024), jnp.int32),
            pltpu.VMEM((512, 1024), BF16),
            pltpu.VMEM((8, 2) + block, F32),
            pltpu.VMEM((4, 4) + block, BF16),
            pltpu.VMEM((4, 4) + block, BF16),
            pltpu.VMEM(block, BF16),
            pltpu.VMEM(block, BF16),
            pltpu.VMEM((4, 4) + block, F32),
            pltpu.VMEM((4, 4) + block, BF16),
            pltpu.VMEM((4, 4) + block, BF16),
            pltpu.VMEM((4, 4) + block, BF16),
            pltpu.VMEM((4, 4) + block, BF16),
            pltpu.VMEM((4,) + block, BF16),
            pltpu.VMEM((4,) + block, BF16),
            pltpu.VMEM((4, W, 384), F32),
            pltpu.VMEM((4, W, 384), F32),
            pltpu.VMEM((4, C, 128), F32),
            pltpu.SemaphoreType.DMA((COPIES,)),
            pltpu.SemaphoreType.DMA((COPIES,)),
            pltpu.SemaphoreType.DMA((3,)),
        ],
        compiler_params=pltpu.CompilerParams(
            collective_id=0, has_side_effects=True, vmem_limit_bytes=60 * 2**20
        ),
    )(text_feats.T, image_feats.T, group_ids.reshape(128, 128), log_scale, bias)
    return (text_grad.T, image_grad)


def solution(mesh):
    placed = (P("dp", "tensor"), P("dp", "tensor"), P(), P(), P())
    return jax.shard_map(
        body,
        mesh=mesh,
        in_specs=placed,
        out_specs=(P("dp", "tensor"), P(("dp", "tensor"), None)),
        check_vma=False,
    )
```

```python
import jax
import jax.numpy as jnp
from jax import lax
from jax.experimental import pallas as pl
from jax.experimental.pallas import tpu as pltpu
from jax.sharding import PartitionSpec as P

MESH = pl.DeviceIdType.MESH
F32 = jnp.float32
BF16 = jnp.bfloat16

D = 1152
W = 32
NT = 16
C = D // NT
COPIES = 84

PLACE = {0: 0, 1: 1, 7: 2, 2: 3, 6: 4, 3: 5, 5: 6, 4: 7}


def device_at(y, z, core, x):
    return (y * 4 + (z // 4) * 2 + core, (z % 4) * 4 + x)


def kernel(
    text_hbm, image_hbm, ids_hbm, log_scale_ref, bias_ref,
    text_out, image_out,
    text_own, image_own, ids, cols_out, cols_in, turned, rows_out, rows_in,
    rows32, text_unit, image_unit,
    txt, img, text_ids, image_ids, slopes,
    text_sum, chain_out, chain_in, pair_out, pair_in,
    image_sum, core_out, core_in, x_out, x_in, z_out, z_in,
    grad_out, grad_in, back_out, back_in,
    send_sem, recv_sem, local_sem,
):
    dp, tensor = lax.axis_index("dp"), lax.axis_index("tensor")
    y, core = dp // 4, dp % 2
    z = ((dp // 2) % 2) * 4 + tensor // 4
    x = tensor % 4
    parity = z % 2

    def along(dy=0, dz=0, dx=0, flip=False):
        return device_at((y + dy) % 8, (z + dz) % 8, (1 - core) if flip else core, (x + dx) % 4)

    z_lo = z % 4
    z_mate = device_at(y, z + 1 - 2 * parity, core, x)
    core_mate = along(flip=True)

    def slant(dy):
        return device_at((y + dy) % 8, z + 1 - 2 * parity, core, x)

    def z_run(k):
        return device_at(y, z - z_lo + (z_lo + k) % 4, core, x)

    copies = []

    def remote(src, dst, device):
        index = len(copies)
        copy = pltpu.make_async_remote_copy(
            src_ref=src, dst_ref=dst, send_sem=send_sem.at[index], recv_sem=recv_sem.at[index],
            device_id=device, device_id_type=MESH,
        )
        copies.append(copy)
        copy.start()
        return copy

    loads = [
        pltpu.make_async_copy(src, dst, local_sem.at[n])
        for n, (src, dst) in enumerate(
            ((text_hbm, text_own), (image_hbm, image_own), (ids_hbm, ids))
        )
    ]
    for load in loads:
        load.start()

    barrier = pltpu.get_barrier_semaphore()
    greeted = [z_run(k) for k in (1, 2, 3)] + [along(dx=k) for k in (1, 2, 3)]
    greeted += [core_mate, along(dy=1), along(dy=7), along(dz=4)]
    greeted += [device_at(y, (z + 2 + 4 * (1 - z_lo // 2)) % 8, core, x)]
    greeted += [slant(1), slant(7)]
    for device in greeted:
        pl.semaphore_signal(barrier, inc=1, device_id=device, device_id_type=MESH)

    for load in loads:
        load.wait()
    for kind, own in enumerate((text_own, image_own)):
        for run in range(4):
            piece = own[:, run * 128 : run * 128 + 128].astype(F32)
            cols_out[kind, run] = jnp.concatenate([piece, jnp.zeros((8, 128), F32)], axis=0).astype(BF16)
    pl.semaphore_wait(barrier, len(greeted))
    run_pieces = []

    def send_run(kind):
        run_pieces.append([
            remote(cols_out.at[kind, (z_lo + k) % 4], cols_in.at[kind, z_lo], z_run(k))
            for k in (1, 3, 2)
        ])
        cols_in[kind, z_lo] = cols_out[kind, z_lo]

    send_run(0)

    def id_row(y_at, z_at, core_at):
        at = (y_at * 4 + (z_at // 4) * 2 + core_at) * 4 + z_at % 4
        return ids[pl.ds(at, 1), :]

    lane = lax.broadcasted_iota(jnp.int32, (W, 128), 1)
    row = lax.broadcasted_iota(jnp.int32, (W, 128), 0)
    own_lane = lane == row + x * W
    for r, place in PLACE.items():
        for p in range(2):
            z_at = z if p == 0 else z + 1 - 2 * parity
            here = jnp.broadcast_to(id_row((y + r) % 8, z_at, core), (W, 128))
            at = (place * 2 + p) * W
            text_ids[at : at + W, :] = jnp.sum(
                jnp.where(own_lane, here, 0), axis=1, keepdims=True
            )
    for c in range(2):
        for q in range(4):
            here = id_row(y, (z + 2 * q) % 8, core if c == 0 else 1 - core)
            from_x = here
            for k in range(1, 4):
                rolled = jnp.concatenate([here[:, k * W :], here[:, : k * W]], axis=1)
                from_x = jnp.where(x == k, rolled, from_x)
            at = (c * 4 + q) * 128
            image_ids[:, at : at + 128] = from_x

    send_run(1)
    scale = jnp.exp(jnp.full((1, 128), log_scale_ref[0], F32))[:, :1]
    offset = bias_ref[0]

    turned[4 * C :, :] = jnp.zeros((384 - 4 * C, 128), F32)
    x_pieces = []
    for kind in range(2):
        for copy in run_pieces[kind]:
            copy.wait_recv()
        for run in range(4):
            turned[run * C : run * C + C, :] = cols_in[kind, run].astype(F32)[:C]
        rows_out[kind] = turned[...].T.astype(BF16).reshape(4, W, 384)
        x_pieces.append([
            remote(rows_out.at[kind, (x + k) % 4], rows_in.at[kind, x], along(dx=k))
            for k in (1, 3, 2)
        ])
        rows_in[kind, x] = rows_out[kind, x]

    def normalize(kind, unit_ref):
        for copy in x_pieces[kind]:
            copy.wait_recv()
        total = jnp.zeros((W, 1), F32)
        for j in range(4):
            wide = rows_in[kind, j].astype(F32)[:, : 4 * C]
            rows32[:, j * 4 * C : (j + 1) * 4 * C] = wide
            total = total + jnp.sum(wide * wide, axis=1, keepdims=True)
        inverse = lax.rsqrt(total + 1e-06)
        unit = rows32[...] * inverse
        unit_ref[...] = unit
        return unit.astype(BF16), inverse

    hat, text_inverse = normalize(0, text_unit)
    txt[0, 0] = hat

    def text_slot(r, p):
        return txt.at[PLACE[r], p]

    def forward(r, p):
        arrive = {}
        if r == 0 or (r > 4 and (r > 5 or p == 0)):
            arrive[(r - 1) % 8] = remote(text_slot(r, p), text_slot((r - 1) % 8, p), along(dy=1))
        if r == 0 or (r < 4 and (r < 3 or p == 1)):
            arrive[r + 1] = remote(text_slot(r, p), text_slot(r + 1, p), along(dy=7))
        return arrive

    waiting = {(r, 0): copy for r, copy in forward(0, 0).items()}

    def text_step(r, p):
        waiting.pop((r, p)).wait_recv()
        waiting.update({(s, p): copy for s, copy in forward(r, p).items()})

    hat, image_inverse = normalize(1, image_unit)
    img[0, 0, 0] = hat
    z_wait = {}
    x_wait = {}
    for q in (1, 3, 2):
        z_wait[q] = remote(img.at[0, 0, 0], img.at[0, q, 0], along(dz=-2 * q))

    def spread_x(q):
        for k in (1, 3, 2):
            x_wait[(q, k)] = remote(img.at[0, q, 0], img.at[0, q, k], along(dx=-k))

    core_wait = {}

    def to_core(q):
        for k in (1, 3, 2):
            x_wait.pop((q, k)).wait_recv()
        core_wait[q] = remote(img.at[0, q], img.at[1, q], core_mate)

    waiting[(7, 1)] = remote(text_slot(0, 0), text_slot(7, 1), slant(1))
    waiting[(1, 1)] = remote(text_slot(0, 0), text_slot(1, 1), slant(7))
    pair = remote(text_slot(0, 0), text_slot(0, 1), z_mate)
    spread_x(0)
    text_step(7, 0)
    text_step(1, 0)
    for q in (1, 3):
        z_wait[q].wait_recv()
        spread_x(q)
    text_step(7, 1)
    text_step(1, 1)
    pair.wait_recv()
    z_wait[2].wait_recv()
    spread_x(2)
    text_step(6, 0)
    text_step(2, 0)
    to_core(0)
    text_step(6, 1)
    text_step(2, 1)
    to_core(1)
    text_step(5, 0)
    text_step(3, 1)
    to_core(3)
    text_step(5, 1)
    text_step(3, 0)
    to_core(2)

    def tile(batch, c, half):
        rows = txt[4 * batch : 4 * batch + 4].reshape(256, D)
        cols = img[c, 2 * half : 2 * half + 2].reshape(256, D)
        at = c * 512 + half * 256
        logits = (
            scale
            * lax.dot_general(rows, cols, (((1,), (1,)), ((), ())), preferred_element_type=F32)
            + offset
        )
        same = text_ids[batch * 256 : batch * 256 + 256, :] == image_ids[:, at : at + 256]
        share = 1.0 / (1.0 + jnp.exp(jnp.where(same, logits, -logits)))
        slopes[batch * 256 : batch * 256 + 256, at : at + 256] = jnp.where(
            same, -share, share
        ).astype(BF16)

    def text_push(batch):
        push = jnp.dot(
            slopes[batch * 256 : batch * 256 + 256, :], img[...].reshape(1024, D),
            preferred_element_type=F32,
        )
        text_sum[4 * batch : 4 * batch + 4] = push.reshape(4, 2, W, D)

    for q in range(4):
        core_wait[q].wait_recv()
    for c in range(2):
        for half in range(2):
            tile(0, c, half)
    text_push(0)
    pair_out[...] = text_sum[0, 1].astype(BF16)
    mate_sum = remote(pair_out, pair_in, z_mate)
    text_step(4, 0)
    text_step(4, 1)
    for c in range(2):
        for half in range(2):
            tile(1, c, half)
    text_push(1)

    chains = (
        (0, 0, (4, 3, 2, 1)),
        (1, 1, (4, 5, 6, 7)),
        (0, 1, (3, 2, 1)),
        (1, 0, (5, 6, 7)),
    )
    arrived = {}

    def chain_step(number, hop):
        way, p, slots = chains[number]
        part = text_sum[PLACE[slots[hop]], p]
        if hop:
            arrived[number].wait_recv()
            part = part + chain_in[number, hop - 1].astype(F32)
        chain_out[number, hop] = part.astype(BF16)
        dy = 1 if way == 0 else 7
        device = slant(dy) if p == 1 and slots[hop] in (1, 7) else along(dy=dy)
        arrived[number] = remote(chain_out.at[number, hop], chain_in.at[number, hop], device)

    chain_step(0, 0)
    chain_step(1, 0)

    def image_push(c, half):
        at = c * 512 + half * 256
        return lax.dot_general(
            slopes[:, at : at + 256], txt[...].reshape(512, D),
            (((0,), (0,)), ((), ())), preferred_element_type=F32,
        ).reshape(2, 4, W, D)

    x_sums = {}
    z_sums = {}

    def x_send(q):
        for k in (2, 1, 3):
            x_out[q, k] = (image_sum[q, k] + core_in[q, k].astype(F32)).astype(BF16)
            x_sums[(q, k)] = remote(x_out.at[q, k], x_in.at[q, k], along(dx=k))

    def z_part(q):
        part = image_sum[q, 0] + core_in[q, 0].astype(F32)
        for k in (2, 1, 3):
            x_sums[(q, k)].wait_recv()
            part = part + x_in[q, k].astype(F32)
        return part

    def z_send(q):
        z_out[q] = z_part(q).astype(BF16)
        z_sums[q] = remote(z_out.at[q], z_in.at[q], along(dz=2 * q))

    core_sums = []
    for half in (1, 0):
        core_out[2 * half : 2 * half + 2] = image_push(1, half).astype(BF16)
        core_sums.append(
            remote(core_out.at[pl.ds(2 * half, 2)], core_in.at[pl.ds(2 * half, 2)], core_mate)
        )
    chain_step(2, 0)
    chain_step(3, 0)
    for half in (1, 0):
        image_sum[2 * half : 2 * half + 2] = image_push(0, half)
    core_sums[0].wait_recv()
    x_send(2)
    chain_step(0, 1)
    chain_step(1, 1)
    x_send(3)
    core_sums[1].wait_recv()
    x_send(1)
    chain_step(2, 1)
    chain_step(3, 1)
    x_send(0)
    chain_step(0, 2)
    chain_step(1, 2)
    chain_step(2, 2)
    chain_step(3, 2)
    z_send(2)
    chain_step(0, 3)
    chain_step(1, 3)
    z_send(3)

    def unit_back(push, unit, inverse):
        push = push * scale
        return (push - unit * jnp.sum(unit * push, axis=1, keepdims=True)) * inverse

    mate_sum.wait_recv()
    push = text_sum[0, 0] + pair_in[...].astype(F32)
    for number in (2, 3, 0, 1):
        arrived[number].wait_recv()
        push = push + chain_in[number, len(chains[number][2]) - 1].astype(F32)
    grad = unit_back(push, text_unit[...], text_inverse)
    blank = jnp.zeros((W, 384 - 4 * C), F32)
    for j in range(4):
        piece = grad[:, j * 4 * C : (j + 1) * 4 * C]
        grad_out[j] = jnp.concatenate([piece, blank], axis=1).astype(BF16)
    x_back = [
        remote(grad_out.at[(x + k) % 4], grad_in.at[x], along(dx=k)) for k in (1, 3, 2)
    ]
    grad_in[x] = grad_out[x]
    z_send(1)
    image_push_total = z_part(0)
    for copy in x_back:
        copy.wait_recv()
    down = grad_in[...].astype(F32).reshape(128, 384).T
    for run in range(4):
        piece = down[run * C : run * C + C]
        back_out[run] = jnp.concatenate([piece, jnp.zeros((8, 128), F32)], axis=0).astype(BF16)
    z_back = [
        remote(back_out.at[(z_lo + k) % 4], back_in.at[z_lo], z_run(k)) for k in (1, 3, 2)
    ]
    back_in[z_lo] = back_out[z_lo]

    for q in (1, 3, 2):
        z_sums[q].wait_recv()
        image_push_total = image_push_total + z_in[q].astype(F32)
    grad = unit_back(image_push_total, image_unit[...], image_inverse)
    for j in range(4):
        for run in range(4):
            at = (j * 4 + run) * C
            image_out[:, (run * 4 + j) * C : (run * 4 + j + 1) * C] = grad[:, at : at + C]

    for copy in z_back:
        copy.wait_recv()
    for run in range(4):
        text_out[:, run * 128 : run * 128 + 128] = back_in[run].astype(F32)[:C]
    for copy in copies:
        copy.wait_send()


def body(text_feats, image_feats, group_ids, log_scale, bias):
    hbm = pl.BlockSpec(memory_space=pltpu.HBM)
    vmem = pl.BlockSpec(memory_space=pltpu.VMEM)
    smem = pl.BlockSpec(memory_space=pltpu.SMEM)
    block = (W, D)
    text_grad, image_grad = pl.pallas_call(
        kernel,
        out_shape=(
            jax.ShapeDtypeStruct((C, NT * W), F32),
            jax.ShapeDtypeStruct(block, F32),
        ),
        in_specs=[hbm, hbm, hbm, smem, smem],
        out_specs=(vmem, vmem),
        scratch_shapes=[
            pltpu.VMEM((C, NT * W), BF16),
            pltpu.VMEM((C, NT * W), BF16),
            pltpu.VMEM((128, 128), jnp.int32),
            pltpu.VMEM((2, 4, C + 8, 128), BF16),
            pltpu.VMEM((2, 4, C + 8, 128), BF16),
            pltpu.VMEM((384, 128), F32),
            pltpu.VMEM((2, 4, W, 384), BF16),
            pltpu.VMEM((2, 4, W, 384), BF16),
            pltpu.VMEM(block, F32),
            pltpu.VMEM(block, F32),
            pltpu.VMEM(block, F32),
            pltpu.VMEM((8, 2) + block, BF16),
            pltpu.VMEM((2, 4, 4) + block, BF16),
            pltpu.VMEM((512, 1), jnp.int32),
            pltpu.VMEM((1, 1024), jnp.int32),
            pltpu.VMEM((512, 1024), BF16),
            pltpu.VMEM((8, 2) + block, F32),
            pltpu.VMEM((4, 4) + block, BF16),
            pltpu.VMEM((4, 4) + block, BF16),
            pltpu.VMEM(block, BF16),
            pltpu.VMEM(block, BF16),
            pltpu.VMEM((4, 4) + block, F32),
            pltpu.VMEM((4, 4) + block, BF16),
            pltpu.VMEM((4, 4) + block, BF16),
            pltpu.VMEM((4, 4) + block, BF16),
            pltpu.VMEM((4, 4) + block, BF16),
            pltpu.VMEM((4,) + block, BF16),
            pltpu.VMEM((4,) + block, BF16),
            pltpu.VMEM((4, W, 384), BF16),
            pltpu.VMEM((4, W, 384), BF16),
            pltpu.VMEM((4, C + 8, 128), BF16),
            pltpu.VMEM((4, C + 8, 128), BF16),
            pltpu.SemaphoreType.DMA((COPIES,)),
            pltpu.SemaphoreType.DMA((COPIES,)),
            pltpu.SemaphoreType.DMA((3,)),
        ],
        compiler_params=pltpu.CompilerParams(
            collective_id=0, has_side_effects=True, vmem_limit_bytes=60 * 2**20
        ),
    )(text_feats.T, image_feats.T, group_ids.reshape(128, 128), log_scale, bias)
    return (text_grad.T, image_grad)


def solution(mesh):
    placed = (P("dp", "tensor"), P("dp", "tensor"), P(), P(), P())
    return jax.shard_map(
        body,
        mesh=mesh,
        in_specs=placed,
        out_specs=(P("dp", "tensor"), P(("dp", "tensor"), None)),
        check_vma=False,
    )
```

```python
import jax
import jax.numpy as jnp
from jax import lax
from jax.experimental import pallas as pl
from jax.experimental.pallas import tpu as pltpu
from jax.sharding import PartitionSpec as P

MESH = pl.DeviceIdType.MESH
F32 = jnp.float32
BF16 = jnp.bfloat16

D = 1152
W = 32
NT = 16
C = D // NT
COPIES = 84

PLACE = {0: 0, 1: 1, 7: 2, 2: 3, 6: 4, 3: 5, 5: 6, 4: 7}


def device_at(y, z, core, x):
    return (y * 4 + (z // 4) * 2 + core, (z % 4) * 4 + x)


def kernel(
    text_hbm, image_hbm, ids_hbm, log_scale_ref, bias_ref,
    text_out, image_out,
    text_own, image_own, ids, cols_out, cols_in, turned, rows_out, rows_in,
    rows32, text_unit, image_unit,
    txt, img, text_ids, image_ids, slopes,
    text_sum, chain_out, chain_in, pair_out, pair_in,
    image_sum, core_out, core_in, x_out, x_in, z_out, z_in,
    grad_out, grad_in, back_out, back_in,
    send_sem, recv_sem, local_sem,
):
    dp, tensor = lax.axis_index("dp"), lax.axis_index("tensor")
    y, core = dp // 4, dp % 2
    z = ((dp // 2) % 2) * 4 + tensor // 4
    x = tensor % 4
    parity = z % 2

    def along(dy=0, dz=0, dx=0, flip=False):
        return device_at((y + dy) % 8, (z + dz) % 8, (1 - core) if flip else core, (x + dx) % 4)

    z_lo = z % 4
    z_mate = device_at(y, z + 1 - 2 * parity, core, x)
    core_mate = along(flip=True)

    def slant(dy):
        return device_at((y + dy) % 8, z + 1 - 2 * parity, core, x)

    def z_run(k):
        return device_at(y, z - z_lo + (z_lo + k) % 4, core, x)

    copies = []

    def remote(src, dst, device):
        index = len(copies)
        copy = pltpu.make_async_remote_copy(
            src_ref=src, dst_ref=dst, send_sem=send_sem.at[index], recv_sem=recv_sem.at[index],
            device_id=device, device_id_type=MESH,
        )
        copies.append(copy)
        copy.start()
        return copy

    loads = [
        pltpu.make_async_copy(src, dst, local_sem.at[n])
        for n, (src, dst) in enumerate(
            ((text_hbm, text_own), (image_hbm, image_own), (ids_hbm, ids))
        )
    ]
    for load in loads:
        load.start()

    barrier = pltpu.get_barrier_semaphore()
    greeted = [z_run(k) for k in (1, 2, 3)] + [along(dx=k) for k in (1, 2, 3)]
    greeted += [core_mate, along(dy=1), along(dy=7), along(dz=4)]
    greeted += [device_at(y, (z + 2 + 4 * (1 - z_lo // 2)) % 8, core, x)]
    greeted += [slant(1), slant(7)]
    for device in greeted:
        pl.semaphore_signal(barrier, inc=1, device_id=device, device_id_type=MESH)

    for load in loads:
        load.wait()
    for kind, own in enumerate((text_own, image_own)):
        for run in range(4):
            piece = own[:, run * 128 : run * 128 + 128].astype(F32)
            cols_out[kind, run] = jnp.concatenate([piece, jnp.zeros((8, 128), F32)], axis=0).astype(BF16)
    pl.semaphore_wait(barrier, len(greeted))
    run_pieces = []

    def send_run(kind):
        run_pieces.append([
            remote(cols_out.at[kind, (z_lo + k) % 4], cols_in.at[kind, z_lo], z_run(k))
            for k in (1, 3, 2)
        ])
        cols_in[kind, z_lo] = cols_out[kind, z_lo]

    send_run(0)

    def id_row(y_at, z_at, core_at):
        at = (y_at * 4 + (z_at // 4) * 2 + core_at) * 4 + z_at % 4
        return ids[pl.ds(at, 1), :]

    lane = lax.broadcasted_iota(jnp.int32, (W, 128), 1)
    row = lax.broadcasted_iota(jnp.int32, (W, 128), 0)
    own_lane = lane == row + x * W
    for r, place in PLACE.items():
        for p in range(2):
            z_at = z if p == 0 else z + 1 - 2 * parity
            here = jnp.broadcast_to(id_row((y + r) % 8, z_at, core), (W, 128))
            at = (place * 2 + p) * W
            text_ids[at : at + W, :] = jnp.sum(
                jnp.where(own_lane, here, 0), axis=1, keepdims=True
            )
    for c in range(2):
        for q in range(4):
            here = id_row(y, (z + 2 * q) % 8, core if c == 0 else 1 - core)
            from_x = here
            for k in range(1, 4):
                rolled = jnp.concatenate([here[:, k * W :], here[:, : k * W]], axis=1)
                from_x = jnp.where(x == k, rolled, from_x)
            at = (c * 4 + q) * 128
            image_ids[:, at : at + 128] = from_x

    send_run(1)
    scale = jnp.exp(jnp.full((1, 128), log_scale_ref[0], F32))[:, :1]
    offset = bias_ref[0]

    turned[4 * C :, :] = jnp.zeros((384 - 4 * C, 128), F32)
    x_pieces = []
    for kind in range(2):
        for copy in run_pieces[kind]:
            copy.wait_recv()
        for run in range(4):
            turned[run * C : run * C + C, :] = cols_in[kind, run].astype(F32)[:C]
        rows_out[kind] = turned[...].T.astype(BF16).reshape(4, W, 384)
        x_pieces.append([
            remote(rows_out.at[kind, (x + k) % 4], rows_in.at[kind, x], along(dx=k))
            for k in (1, 3, 2)
        ])
        rows_in[kind, x] = rows_out[kind, x]

    def normalize(kind, unit_ref):
        for copy in x_pieces[kind]:
            copy.wait_recv()
        total = jnp.zeros((W, 1), F32)
        for j in range(4):
            wide = rows_in[kind, j].astype(F32)[:, : 4 * C]
            rows32[:, j * 4 * C : (j + 1) * 4 * C] = wide
            total = total + jnp.sum(wide * wide, axis=1, keepdims=True)
        inverse = lax.rsqrt(total + 1e-06)
        unit = rows32[...] * inverse
        unit_ref[...] = unit
        return unit.astype(BF16), inverse

    hat, text_inverse = normalize(0, text_unit)
    txt[0, 0] = hat

    def text_slot(r, p):
        return txt.at[PLACE[r], p]

    def forward(r, p):
        arrive = {}
        if r == 0 or (r > 4 and (r > 5 or p == 0)):
            arrive[(r - 1) % 8] = remote(text_slot(r, p), text_slot((r - 1) % 8, p), along(dy=1))
        if r == 0 or (r < 4 and (r < 3 or p == 1)):
            arrive[r + 1] = remote(text_slot(r, p), text_slot(r + 1, p), along(dy=7))
        return arrive

    waiting = {(r, 0): copy for r, copy in forward(0, 0).items()}

    def text_step(r, p):
        waiting.pop((r, p)).wait_recv()
        waiting.update({(s, p): copy for s, copy in forward(r, p).items()})

    hat, image_inverse = normalize(1, image_unit)
    img[0, 0, 0] = hat
    z_wait = {}
    x_wait = {}
    for q in (1, 3, 2):
        z_wait[q] = remote(img.at[0, 0, 0], img.at[0, q, 0], along(dz=-2 * q))

    def spread_x(q):
        for k in (1, 3, 2):
            x_wait[(q, k)] = remote(img.at[0, q, 0], img.at[0, q, k], along(dx=-k))

    core_wait = {}

    def to_core(q):
        for k in (1, 3, 2):
            x_wait.pop((q, k)).wait_recv()
        core_wait[q] = remote(img.at[0, q], img.at[1, q], core_mate)

    waiting[(7, 1)] = remote(text_slot(0, 0), text_slot(7, 1), slant(1))
    waiting[(1, 1)] = remote(text_slot(0, 0), text_slot(1, 1), slant(7))
    pair = remote(text_slot(0, 0), text_slot(0, 1), z_mate)
    spread_x(0)
    text_step(7, 0)
    text_step(1, 0)
    for q in (1, 3):
        z_wait[q].wait_recv()
        spread_x(q)
    text_step(7, 1)
    text_step(1, 1)
    pair.wait_recv()
    z_wait[2].wait_recv()
    spread_x(2)
    text_step(6, 0)
    text_step(2, 0)
    to_core(0)
    text_step(6, 1)
    text_step(2, 1)
    to_core(1)
    text_step(5, 0)
    text_step(3, 1)
    to_core(3)
    text_step(5, 1)
    text_step(3, 0)
    to_core(2)

    gather_copies = len(copies)

    def tile(batch, c, half):
        rows = txt[4 * batch : 4 * batch + 4].reshape(256, D)
        cols = img[c, 2 * half : 2 * half + 2].reshape(256, D)
        at = c * 512 + half * 256
        logits = (
            scale
            * lax.dot_general(rows, cols, (((1,), (1,)), ((), ())), preferred_element_type=F32)
            + offset
        )
        same = text_ids[batch * 256 : batch * 256 + 256, :] == image_ids[:, at : at + 256]
        share = 1.0 / (1.0 + jnp.exp(jnp.where(same, logits, -logits)))
        slopes[batch * 256 : batch * 256 + 256, at : at + 256] = jnp.where(
            same, -share, share
        ).astype(BF16)

    def text_push(batch):
        push = jnp.dot(
            slopes[batch * 256 : batch * 256 + 256, :], img[...].reshape(1024, D),
            preferred_element_type=F32,
        )
        text_sum[4 * batch : 4 * batch + 4] = push.reshape(4, 2, W, D)

    for q in range(4):
        core_wait[q].wait_recv()
    for c in range(2):
        for half in range(2):
            tile(0, c, half)
    text_push(0)
    pair_out[...] = text_sum[0, 1].astype(BF16)
    mate_sum = remote(pair_out, pair_in, z_mate)
    text_step(4, 0)
    text_step(4, 1)
    for c in range(2):
        for half in range(2):
            tile(1, c, half)
    text_push(1)

    chains = (
        (0, 0, (4, 3, 2, 1)),
        (1, 1, (4, 5, 6, 7)),
        (0, 1, (3, 2, 1)),
        (1, 0, (5, 6, 7)),
    )
    arrived = {}

    def chain_step(number, hop):
        way, p, slots = chains[number]
        part = text_sum[PLACE[slots[hop]], p]
        if hop:
            arrived[number].wait_recv()
            part = part + chain_in[number, hop - 1].astype(F32)
        chain_out[number, hop] = part.astype(BF16)
        dy = 1 if way == 0 else 7
        device = slant(dy) if p == 1 and slots[hop] in (1, 7) else along(dy=dy)
        arrived[number] = remote(chain_out.at[number, hop], chain_in.at[number, hop], device)

    chain_step(0, 0)
    chain_step(1, 0)

    def image_push(c, half):
        at = c * 512 + half * 256
        return lax.dot_general(
            slopes[:, at : at + 256], txt[...].reshape(512, D),
            (((0,), (0,)), ((), ())), preferred_element_type=F32,
        ).reshape(2, 4, W, D)

    x_sums = {}
    z_sums = {}

    def x_send(q):
        for k in (2, 1, 3):
            x_out[q, k] = (image_sum[q, k] + core_in[q, k].astype(F32)).astype(BF16)
            x_sums[(q, k)] = remote(x_out.at[q, k], x_in.at[q, k], along(dx=k))

    def z_part(q):
        part = image_sum[q, 0] + core_in[q, 0].astype(F32)
        for k in (2, 1, 3):
            x_sums[(q, k)].wait_recv()
            part = part + x_in[q, k].astype(F32)
        return part

    def z_send(q):
        z_out[q] = z_part(q).astype(BF16)
        z_sums[q] = remote(z_out.at[q], z_in.at[q], along(dz=2 * q))

    core_sums = []
    for half in (1, 0):
        core_out[2 * half : 2 * half + 2] = image_push(1, half).astype(BF16)
        core_sums.append(
            remote(core_out.at[pl.ds(2 * half, 2)], core_in.at[pl.ds(2 * half, 2)], core_mate)
        )
    chain_step(2, 0)
    chain_step(3, 0)
    for half in (1, 0):
        image_sum[2 * half : 2 * half + 2] = image_push(0, half)
    for copy in copies[:gather_copies]:
        copy.wait_send()
    core_sums[0].wait_recv()
    x_send(2)
    chain_step(0, 1)
    chain_step(1, 1)
    x_send(3)
    core_sums[1].wait_recv()
    x_send(1)
    chain_step(2, 1)
    chain_step(3, 1)
    x_send(0)
    chain_step(0, 2)
    chain_step(1, 2)
    chain_step(2, 2)
    chain_step(3, 2)
    z_send(2)
    chain_step(0, 3)
    chain_step(1, 3)
    z_send(3)

    def unit_back(push, unit, inverse):
        push = push * scale
        return (push - unit * jnp.sum(unit * push, axis=1, keepdims=True)) * inverse

    mate_sum.wait_recv()
    push = text_sum[0, 0] + pair_in[...].astype(F32)
    for number in (2, 3, 0, 1):
        arrived[number].wait_recv()
        push = push + chain_in[number, len(chains[number][2]) - 1].astype(F32)
    grad = unit_back(push, text_unit[...], text_inverse)
    blank = jnp.zeros((W, 384 - 4 * C), F32)
    for j in range(4):
        piece = grad[:, j * 4 * C : (j + 1) * 4 * C]
        grad_out[j] = jnp.concatenate([piece, blank], axis=1).astype(BF16)
    x_back = [
        remote(grad_out.at[(x + k) % 4], grad_in.at[x], along(dx=k)) for k in (1, 3, 2)
    ]
    grad_in[x] = grad_out[x]
    z_send(1)
    image_push_total = z_part(0)
    for copy in x_back:
        copy.wait_recv()
    down = grad_in[...].astype(F32).reshape(128, 384).T
    for run in range(4):
        piece = down[run * C : run * C + C]
        back_out[run] = jnp.concatenate([piece, jnp.zeros((8, 128), F32)], axis=0).astype(BF16)
    z_back = [
        remote(back_out.at[(z_lo + k) % 4], back_in.at[z_lo], z_run(k)) for k in (1, 3, 2)
    ]
    back_in[z_lo] = back_out[z_lo]

    for q in (1, 3, 2):
        z_sums[q].wait_recv()
        image_push_total = image_push_total + z_in[q].astype(F32)
    grad = unit_back(image_push_total, image_unit[...], image_inverse)
    for j in range(4):
        for run in range(4):
            at = (j * 4 + run) * C
            image_out[:, (run * 4 + j) * C : (run * 4 + j + 1) * C] = grad[:, at : at + C]

    for copy in copies[gather_copies:]:
        copy.wait_send()
    for copy in z_back:
        copy.wait_recv()
    for run in range(4):
        text_out[:, run * 128 : run * 128 + 128] = back_in[run].astype(F32)[:C]


def body(text_feats, image_feats, group_ids, log_scale, bias):
    hbm = pl.BlockSpec(memory_space=pltpu.HBM)
    vmem = pl.BlockSpec(memory_space=pltpu.VMEM)
    smem = pl.BlockSpec(memory_space=pltpu.SMEM)
    block = (W, D)
    text_grad, image_grad = pl.pallas_call(
        kernel,
        out_shape=(
            jax.ShapeDtypeStruct((C, NT * W), F32),
            jax.ShapeDtypeStruct(block, F32),
        ),
        in_specs=[hbm, hbm, hbm, smem, smem],
        out_specs=(vmem, vmem),
        scratch_shapes=[
            pltpu.VMEM((C, NT * W), BF16),
            pltpu.VMEM((C, NT * W), BF16),
            pltpu.VMEM((128, 128), jnp.int32),
            pltpu.VMEM((2, 4, C + 8, 128), BF16),
            pltpu.VMEM((2, 4, C + 8, 128), BF16),
            pltpu.VMEM((384, 128), F32),
            pltpu.VMEM((2, 4, W, 384), BF16),
            pltpu.VMEM((2, 4, W, 384), BF16),
            pltpu.VMEM(block, F32),
            pltpu.VMEM(block, F32),
            pltpu.VMEM(block, F32),
            pltpu.VMEM((8, 2) + block, BF16),
            pltpu.VMEM((2, 4, 4) + block, BF16),
            pltpu.VMEM((512, 1), jnp.int32),
            pltpu.VMEM((1, 1024), jnp.int32),
            pltpu.VMEM((512, 1024), BF16),
            pltpu.VMEM((8, 2) + block, F32),
            pltpu.VMEM((4, 4) + block, BF16),
            pltpu.VMEM((4, 4) + block, BF16),
            pltpu.VMEM(block, BF16),
            pltpu.VMEM(block, BF16),
            pltpu.VMEM((4, 4) + block, F32),
            pltpu.VMEM((4, 4) + block, BF16),
            pltpu.VMEM((4, 4) + block, BF16),
            pltpu.VMEM((4, 4) + block, BF16),
            pltpu.VMEM((4, 4) + block, BF16),
            pltpu.VMEM((4,) + block, BF16),
            pltpu.VMEM((4,) + block, BF16),
            pltpu.VMEM((4, W, 384), BF16),
            pltpu.VMEM((4, W, 384), BF16),
            pltpu.VMEM((4, C + 8, 128), BF16),
            pltpu.VMEM((4, C + 8, 128), BF16),
            pltpu.SemaphoreType.DMA((COPIES,)),
            pltpu.SemaphoreType.DMA((COPIES,)),
            pltpu.SemaphoreType.DMA((3,)),
        ],
        compiler_params=pltpu.CompilerParams(
            collective_id=0, has_side_effects=True, vmem_limit_bytes=60 * 2**20
        ),
    )(text_feats.T, image_feats.T, group_ids.reshape(128, 128), log_scale, bias)
    return (text_grad.T, image_grad)


def solution(mesh):
    placed = (P("dp", "tensor"), P("dp", "tensor"), P(), P(), P())
    return jax.shard_map(
        body,
        mesh=mesh,
        in_specs=placed,
        out_specs=(P("dp", "tensor"), P(("dp", "tensor"), None)),
        check_vma=False,
    )
```
